32 devices in a mesh: blk: 8 (over z, y), grp: 4 (over x, core).
Axes of the slice: x: 2, y: 2, z: 4, core: 2. Of those that a mesh axis runs over, the one named last changes fastest.
Arguments:
- images: bfloat16 [2048, 1536], P('blk'), may hold values from -100 to 100
- defocus: float32 [2048], P('blk'), may hold values from 1 to 12
- class_id: int32 [2048, 1], P('blk'), may hold values from 0 to 63; in each aligned block of 256 rows (0 to 255, 256 to 511, ...) at most 10 rows name the same one
- rotation_id: int32 [2048], P('blk'), may hold values from 0 to 31
- shift_id: int32 [2048], P('blk'), may hold values from 0 to 8
- references: float32 [4, 16, 1536], P('grp', 'blk'), may hold values from -4 to 4
- owner: int32 [4, 16], P('grp'), may hold values from 0 to 15, as said below
- inv_noise: float32 [24], replicated, may hold values from 0.5 to 2
- prior: float32 [24], replicated, may hold values from 0.5 to 2
Outputs:
- evidence: float32 [2048], P('blk')
- new_refs: float32 [4, 16, 1536], P('grp', 'blk')
The draws below stay inside these ranges and needn't reach their ends.
Inputs may be any that keep to these rules, and one draw needn't show every extreme that they name: `class_id`: among the particles of one index of blk, no class is assigned to more than 10 particles, and some class to exactly 10. `owner`: each row is a permutation of 0 to 15.
All inputs are finite; a program needn't handle non-finite values.
Results may differ from the reference program's by a relative error of at most 0.0036.
Values sent between devices are 32-bit elements; how exact they have to be, the bound alone decides.
A program may use at most 64 MiB of HBM per device.

```python
import math
import jax
import jax.numpy as jnp
import numpy as np
from jax import lax

CYCLES = 24
ANGLES = 32
SHIFTS = 9
CL_DEV = 2
P_BLK = 256
FEAT = 1536
C_GRP = 16
GROUPS = 4
CLASSES = 64
PARTICLES = 2048
MOST = 10


def draw_owner(key, part):
    row_keys = jax.random.split(key, GROUPS)

    def one_row(row_key):
        return jax.random.permutation(row_key, C_GRP)
    return jax.vmap(one_row)(row_keys).astype(jnp.int32)


def rough_values(key, shape):
    return jnp.clip(jax.random.normal(key, shape, jnp.float32), -4.0, 4.0)


def place_template(pattern, turned, moved):
    angular = jnp.arange(ANGLES, dtype=jnp.int32)
    source = (angular[None, :] - turned[:, None]) % ANGLES
    rotated = jnp.take_along_axis(pattern, jnp.broadcast_to(source[:, None, None, :], pattern.shape), axis=3)
    radius = (jnp.arange(CYCLES, dtype=jnp.float32) + 1.0) / (2.0 * CYCLES)
    bearing = 2.0 * math.pi / ANGLES * jnp.arange(ANGLES, dtype=jnp.float32)
    shift_x = (moved // 3 - 1).astype(jnp.float32)
    shift_y = (moved % 3 - 1).astype(jnp.float32)
    along = shift_x[:, None] * jnp.cos(bearing)[None, :] + shift_y[:, None] * jnp.sin(bearing)[None, :]
    phase = -2.0 * math.pi * radius[None, :, None] * along[:, None, :]
    phase_cos = jnp.cos(phase)
    phase_sin = jnp.sin(phase)
    real_part = phase_cos * rotated[:, 0] - phase_sin * rotated[:, 1]
    imag_part = phase_sin * rotated[:, 0] + phase_cos * rotated[:, 1]
    return jnp.stack([real_part, imag_part], axis=1)


def shared_fields(key):
    focus_key = jax.random.fold_in(key, 101)
    class_key = jax.random.fold_in(key, 102)
    noise_key = jax.random.fold_in(key, 103)
    choice_key = jax.random.fold_in(key, 104)
    faint_key = jax.random.fold_in(key, 105)
    defocus = jnp.exp(jax.random.uniform(focus_key, (PARTICLES,), jnp.float32, 0.0, math.log(12.0)))
    defocus = jnp.clip(defocus, 1.0, 12.0)
    references = rough_values(class_key, (GROUPS, C_GRP, FEAT))
    noise = rough_values(noise_key, (PARTICLES, FEAT))
    sample_keys = jax.random.split(choice_key, 8)
    chosen = jax.random.randint(sample_keys[0], (PARTICLES,), 0, 8) == 0
    picked_class = jax.random.randint(sample_keys[1], (PARTICLES,), 0, CLASSES)
    first_turn = jax.random.randint(sample_keys[2], (PARTICLES,), 0, ANGLES)
    second_turn = (first_turn + jax.random.randint(sample_keys[3], (PARTICLES,), 1, ANGLES)) % ANGLES
    first_move = jax.random.randint(sample_keys[4], (PARTICLES,), 0, SHIFTS)
    second_move = jax.random.randint(sample_keys[5], (PARTICLES,), 0, SHIFTS)
    boost = max(1.0, 40.0 / math.sqrt(FEAT))
    bright = boost * jax.random.uniform(sample_keys[6], (PARTICLES,), jnp.float32, 3.0, 12.0)
    faint = boost * jax.random.uniform(faint_key, (PARTICLES,), jnp.float32, 0.3, 0.6)
    strength = jnp.where(chosen, bright, faint)
    second_strength = strength - boost * jax.random.uniform(sample_keys[7], (PARTICLES,), jnp.float32, 0.08, 0.15)
    frequency = (jnp.arange(CYCLES, dtype=jnp.float32) + 1.0) / CYCLES
    contrast = -jnp.sin(defocus[:, None] * (frequency * frequency)[None, :] + 0.15)
    pattern = references.reshape(CLASSES, 2, CYCLES, ANGLES)[picked_class]
    first_view = place_template(pattern, first_turn, first_move)
    second_view = place_template(pattern, second_turn, second_move)
    signal = strength[:, None, None, None] * first_view + second_strength[:, None, None, None] * second_view
    signal = signal * contrast[:, None, :, None]
    images = jnp.clip(noise + signal.reshape(PARTICLES, FEAT), -100.0, 100.0)
    return (defocus, references, images)


def draw_defocus(key, part):
    return shared_fields(key)[0].astype(jnp.float32)


def draw_references(key, part):
    return shared_fields(key)[1].astype(jnp.float32)


def draw_images(key, part):
    return shared_fields(key)[2].astype(jnp.bfloat16)


def touch_ends(values, rng, least, largest):
    index_at = [jax.random.randint(jax.random.fold_in(rng, axis), (), 0, length) for axis, length in enumerate(values.shape)]
    longest = values.shape.index(max(values.shape))
    beside = index_at[:longest] + [(index_at[longest] + 1) % values.shape[longest]] + index_at[longest + 1:]
    return values.at[tuple(index_at)].set(least).at[tuple(beside)].set(largest)


def routed_block(key, own, number, rows, amount, top, most, lean):
    ranking = jax.random.permutation(key, amount)
    heavy_load, usual = load_shares(amount, rows * top, most, lean, True), load_shares(amount, rows * top, most, lean, False)
    places = jnp.arange(amount)

    def named(sizes, rotation):
        used = int((sizes > 0).sum())
        fixed = max(1, used // 4)
        shifted = fixed + (places - fixed + rotation * (used - fixed)) % max(1, amount - fixed)
        return jnp.zeros((amount,), jnp.int32).at[ranking[jnp.where(places < fixed, places, shifted)]].set(jnp.asarray(sizes, jnp.int32))

    sizes = jnp.where(number % 4 == 0, named(heavy_load, number // 4), named(usual, number - number // 4 - 1))
    mixed = jax.random.permutation(jax.random.fold_in(own, 3), amount)
    source_of, sink = mixed[0:amount // 2 * 2:2], mixed[1:amount // 2 * 2:2]
    room = jnp.minimum(sizes[source_of] - 1, most - sizes[sink]) // 2
    room = jnp.where((source_of == ranking[0]) | (sink == ranking[0]) | (sizes[sink] == 0), 0, jnp.maximum(room, 0))
    shifted = jax.random.randint(jax.random.fold_in(own, 4), (amount // 2,), 0, 1 << 20) % (room + 1)
    sizes = sizes.at[source_of].add(-shifted).at[sink].add(shifted)
    members = jnp.searchsorted(jnp.cumsum(sizes), jnp.arange(rows * top), side="right").astype(jnp.int32)
    listing = members.reshape(top, rows).T
    listing = listing[jax.random.permutation(jax.random.fold_in(own, 1), rows)]
    rotation = jax.random.randint(jax.random.fold_in(own, 2), (rows, 1), 0, top)
    return jnp.take_along_axis(listing, (jnp.arange(top)[None, :] + rotation) % top, axis=1)


def load_shares(amount, total, most, lean, full):
    weights = [(1 << 20) // math.isqrt(rank ** lean) + 1 for rank in range(1, amount + 1)]
    largest = most if full else min(most, max(-(-total // amount), total * weights[0] // sum(weights)))
    least = 1 if total - largest >= amount - 1 else 0
    holding, surplus = [largest] + [least] * (amount - 1), total - largest - least * (amount - 1)
    while surplus > 0:
        free = [i for i in range(1, amount) if holding[i] < largest] or [i for i in range(1, amount) if holding[i] < most]
        whole, budget = sum([weights[i] for i in free]), surplus
        for i in free:
            extra = min(most - holding[i], max(1, budget * weights[i] // whole), surplus)
            holding[i] = holding[i] + extra
            surplus = surplus - extra
    return np.array(holding)


def setup_inputs(seed: int = 0) -> dict:
    splits = jax.random.split(jax.random.key(seed), 10)
    images = draw_images(jax.random.fold_in(splits[9], 71), 0)
    defocus = draw_defocus(jax.random.fold_in(splits[9], 71), 0)
    class_id_keys = jax.random.split(jax.random.fold_in(splits[2], 1), PARTICLES // P_BLK)
    class_id_turns = jax.random.permutation(jax.random.fold_in(splits[2], 3), PARTICLES // P_BLK)
    class_id = jax.vmap(lambda own, number: routed_block(jax.random.fold_in(splits[2], 2), own, number, P_BLK, CLASSES, 1, MOST, 3))(class_id_keys, class_id_turns).reshape((PARTICLES, 1))
    rotation_id = touch_ends(jax.random.randint(splits[3], (PARTICLES,), 0, ANGLES), jax.random.fold_in(splits[3], 1), 0, ANGLES - 1).astype(jnp.int32)
    shift_id = touch_ends(jax.random.randint(splits[4], (PARTICLES,), 0, SHIFTS), jax.random.fold_in(splits[4], 1), 0, SHIFTS - 1).astype(jnp.int32)
    references = draw_references(jax.random.fold_in(splits[9], 71), 0)
    owner = draw_owner(jax.random.fold_in(splits[9], 71), 0)
    inv_noise = jnp.clip(jnp.exp(jax.random.uniform(splits[7], (CYCLES,), jnp.float32, math.log(0.5), math.log(2.0))), 0.5, 2.0)
    prior = jnp.clip(jnp.exp(jax.random.uniform(splits[8], (CYCLES,), jnp.float32, math.log(0.5), math.log(2.0))), 0.5, 2.0)
    return {"images": images, "defocus": defocus, "class_id": class_id, "rotation_id": rotation_id, "shift_id": shift_id, "references": references, "owner": owner, "inv_noise": inv_noise, "prior": prior}


def contrast_table(defocus):
    frequency = (jnp.arange(CYCLES, dtype=jnp.float32) + 1.0) / CYCLES
    return -jnp.sin(defocus[:, None] * (frequency * frequency)[None, :] + 0.15)

def phase_tables():
    radius = (jnp.arange(CYCLES, dtype=jnp.float32) + 1.0) / (2.0 * CYCLES)
    bearing = 2.0 * math.pi / ANGLES * jnp.arange(ANGLES, dtype=jnp.float32)
    shift_index = jnp.arange(SHIFTS, dtype=jnp.int32)
    shift_x = (shift_index // 3 - 1).astype(jnp.float32)
    shift_y = (shift_index % 3 - 1).astype(jnp.float32)
    along = shift_x[:, None] * jnp.cos(bearing)[None, :] + shift_y[:, None] * jnp.sin(bearing)[None, :]
    phase = -2.0 * math.pi * radius[None, :, None] * along[:, None, :]
    return (jnp.cos(phase), jnp.sin(phase))

def weigh(images, factor):
    row_total = images.shape[0]
    grid = images.astype(jnp.float32).reshape(row_total, 2, CYCLES, ANGLES)
    return (grid * factor[:, None, :, None]).reshape(row_total, -1).astype(jnp.bfloat16)

def make_templates(ref_block):
    block_rows = ref_block.shape[0]
    grid = ref_block.reshape(block_rows, 2, CYCLES, ANGLES)
    angular = jnp.arange(ANGLES, dtype=jnp.int32)
    turning = (angular[:, None, None] == (angular[None, None, :] - angular[None, :, None]) % ANGLES).astype(jnp.float32)
    rotated = jnp.einsum('nqka,arb->nrqkb', grid, turning, precision=lax.Precision.HIGHEST)
    phase_cos, phase_sin = phase_tables()
    rotated_re = rotated[:, :, 0][:, :, None]
    rotated_im = rotated[:, :, 1][:, :, None]
    real_part = phase_cos[None, None] * rotated_re - phase_sin[None, None] * rotated_im
    imag_part = phase_sin[None, None] * rotated_re + phase_cos[None, None] * rotated_im
    stacked = jnp.stack([real_part, imag_part], axis=3)
    return stacked.reshape(block_rows * ANGLES * SHIFTS, -1).astype(jnp.bfloat16)

def score_block(ref_block, weighted, contrast_power, score_scale):
    block_rows = ref_block.shape[0]
    templates = make_templates(ref_block)
    cross = lax.dot_general(templates, weighted, (((1,), (1,)), ((), ())), preferred_element_type=jnp.float32)
    grid = ref_block.reshape(block_rows, 2, CYCLES, ANGLES)
    power = lax.optimization_barrier(jnp.sum(grid * grid, axis=(1, 3)))
    penalty = jnp.dot(power, contrast_power.T, precision=lax.Precision.HIGHEST)
    logits = (cross.reshape(block_rows, ANGLES * SHIFTS, -1) - 0.5 * penalty[:, None, :]) * score_scale
    return logits.reshape(block_rows * ANGLES * SHIFTS, -1)

def target_rows(relative, rotation_id, shift_id):
    inside = (relative >= 0) & (relative < CL_DEV)
    return jnp.where(inside, (relative * ANGLES + rotation_id) * SHIFTS + shift_id, -1).astype(jnp.int32)

def update(running, logits, target):
    peak, total, picked = running
    new_peak = jnp.maximum(peak, lax.optimization_barrier(jnp.max(logits, axis=0)))
    total = total * jnp.exp(peak - new_peak) + lax.optimization_barrier(jnp.sum(jnp.exp(logits - new_peak[None, :]), axis=0))
    row_index = jnp.arange(logits.shape[0], dtype=jnp.int32)
    picked = picked + lax.optimization_barrier(jnp.sum(jnp.where(row_index[:, None] == target[None, :], logits, 0.0), axis=0))
    return (new_peak, total, picked)

def align_terms(images, contrast, weight, rotation_id, shift_id):
    row_total = images.shape[0]
    phase_cos, phase_sin = phase_tables()
    chosen = (shift_id[:, None] == jnp.arange(SHIFTS, dtype=jnp.int32)[None, :]).astype(jnp.float32)
    cos_rows = jnp.dot(chosen, phase_cos.reshape(SHIFTS, -1), precision=lax.Precision.HIGHEST).reshape(row_total, CYCLES, ANGLES)
    sin_rows = jnp.dot(chosen, phase_sin.reshape(SHIFTS, -1), precision=lax.Precision.HIGHEST).reshape(row_total, CYCLES, ANGLES)
    grid = images.astype(jnp.float32).reshape(row_total, 2, CYCLES, ANGLES)
    unshift_re = cos_rows * grid[:, 0] + sin_rows * grid[:, 1]
    unshift_im = cos_rows * grid[:, 1] - sin_rows * grid[:, 0]
    unshifted = jnp.stack([unshift_re, unshift_im], axis=1)
    angular = jnp.arange(ANGLES, dtype=jnp.int32)
    turning = (angular[None, :, None] == (angular[None, None, :] + rotation_id[:, None, None]) % ANGLES).astype(jnp.float32)
    aligned = jnp.einsum('pqka,pab->pqkb', unshifted, turning, precision=lax.Precision.HIGHEST)
    scaled = weight[:, None] * contrast
    numer_term = (aligned * scaled[:, None, :, None]).reshape(row_total, -1)
    denom_term = weight[:, None] * contrast * contrast
    return (numer_term, denom_term)

def finish(numerator, denominator, prior):
    grid = numerator.reshape(-1, 2, CYCLES, ANGLES)
    return (grid / (denominator + prior[None, :])[:, None, :, None]).reshape(numerator.shape)

def reference(images, defocus, class_id, rotation_id, shift_id, references, owner, inv_noise, prior):
    contrast = contrast_table(defocus)
    contrast_power = contrast * contrast * inv_noise[None, :]
    weighted = weigh(images, contrast * inv_noise[None, :])
    score_scale = 1.0 / math.sqrt(FEAT)
    labels = class_id[:, 0]
    blocks = references.reshape(CLASSES // CL_DEV, CL_DEV, FEAT)
    firsts = CL_DEV * jnp.arange(CLASSES // CL_DEV, dtype=jnp.int32)

    def visit(running, entries):
        ref_block, block_first = entries
        logits = score_block(ref_block, weighted, contrast_power, score_scale)
        return (update(running, logits, target_rows(labels - block_first, rotation_id, shift_id)), None)
    initial = (jnp.full((PARTICLES,), -1e+30, jnp.float32), jnp.zeros((PARTICLES,), jnp.float32), jnp.zeros((PARTICLES,), jnp.float32))
    (peak, total, picked), unused = lax.scan(visit, initial, (blocks, firsts))
    log_orients = math.log(CLASSES * ANGLES * SHIFTS)
    log_sum = peak + jnp.log(total)
    evidence = log_sum - log_orients
    weight = jnp.exp(picked - log_sum + log_orients)
    numer_term, denom_term = align_terms(images, contrast, weight, rotation_id, shift_id)
    slots = (labels // C_GRP * C_GRP + owner.reshape(-1)[labels]).astype(jnp.int32)
    numerator = jax.ops.segment_sum(numer_term, slots, num_segments=CLASSES)
    denominator = jax.ops.segment_sum(denom_term, slots, num_segments=CLASSES)
    new_refs = finish(numerator, denominator, prior).reshape(GROUPS, C_GRP, FEAT)
    return (evidence, new_refs)
```

```python
import functools
import math

import jax
import jax.numpy as jnp
import numpy as np
from jax import lax
from jax.experimental import pallas as pl
from jax.experimental.pallas import tpu as pltpu
from jax.sharding import PartitionSpec as P

CYCLES = 24
ANGLES = 32
SHIFTS = 9
HALF = CYCLES * ANGLES
FEAT = 2 * HALF
LANES = 128
CHUNKS = FEAT // LANES
FOLDED = HALF // 2
FOLDS = FOLDED // LANES
BEND = ANGLES // 2
PAIRS = ((0, 8), (1, 7), (2, 6), (3, 5))
MESH = pl.DeviceIdType.MESH
F32 = jnp.float32
BF16 = jnp.bfloat16
NT = (((1,), (1,)), ((), ()))


def phase_numpy():
    radius = (np.arange(CYCLES) + 1.0) / (2.0 * CYCLES)
    bearing = 2.0 * math.pi / ANGLES * np.arange(ANGLES)
    index = np.arange(SHIFTS)
    shift_x = (index // 3 - 1).astype(np.float64)
    shift_y = (index % 3 - 1).astype(np.float64)
    along = shift_x[:, None] * np.cos(bearing) + shift_y[:, None] * np.sin(bearing)
    phase = (-2.0 * math.pi * radius[None, :, None] * along[:, None, :]).reshape(SHIFTS, HALF)
    return np.cos(phase).astype(np.float32), np.sin(phase).astype(np.float32)


def split_numpy(values):
    high = values.astype(jnp.bfloat16)
    rest = values - high.astype(np.float32)
    middle = rest.astype(jnp.bfloat16)
    low = (rest - middle.astype(np.float32)).astype(jnp.bfloat16)
    return high, middle, low


def constant_tables():
    phase_cos, phase_sin = phase_numpy()
    firsts = [first for first, second in PAIRS]
    pair_rows = np.concatenate([phase_cos[firsts], phase_sin[firsts]], axis=0)
    low_lane = np.arange(FOLDED) % ANGLES < BEND
    pair_rows = np.where(low_lane, pair_rows[:, :FOLDED], pair_rows[:, FOLDED:])
    both = np.concatenate([phase_cos, phase_sin], axis=1)
    chosen_rows = np.zeros((LANES, FEAT), jnp.bfloat16)
    for part, piece in enumerate(split_numpy(both)):
        chosen_rows[part * 16 : part * 16 + SHIFTS] = piece
    spread = np.zeros((LANES, HALF), jnp.bfloat16)
    for part in range(3):
        for k in range(CYCLES):
            spread[part * 32 + k, k * ANGLES : (k + 1) * ANGLES] = 1
    turn = np.zeros((LANES, 8 * LANES), jnp.bfloat16)
    lane = np.arange(LANES)
    for r in range(8):
        turn[lane // ANGLES * ANGLES + (lane - r) % ANGLES, r * LANES + lane] = 1
    bend = np.zeros((LANES, 2 * BEND * LANES), jnp.bfloat16)
    for r in range(BEND):
        source = lane // BEND * BEND + (lane - r) % BEND
        bend[source, r * LANES + lane] = 1
        bend[source, (BEND + r) * LANES + lane] = np.where(lane % BEND < r, -1, 1)
    return pair_rows, chosen_rows, spread, turn, bend


def split3(values):
    high = values.astype(BF16)
    rest = values - high.astype(F32)
    middle = rest.astype(BF16)
    low = (rest - middle.astype(F32)).astype(BF16)
    return high, middle, low


def widen(values, spread):
    high, middle, low = split3(values)
    packed = (
        high.astype(F32)
        + pltpu.roll(middle.astype(F32), 32, 1)
        + pltpu.roll(low.astype(F32), 64, 1)
    )
    return jnp.dot(packed.astype(BF16), spread, preferred_element_type=F32)


def turn_left(values, step, lane):
    near = pltpu.roll(values, LANES - step, 1)
    far = pltpu.roll(values, ANGLES - step, 1)
    return jnp.where(lane % ANGLES < ANGLES - step, near, far)


def fold_half(first, second, lane):
    low = lane % ANGLES < BEND
    here = jnp.where(low, first, second)
    there = turn_left(jnp.where(low, second, first), BEND, lane)
    return here + there, here - there


def kernel(blk_size, grp_size, *refs):
    hbm = refs[:14]
    refs_hbm = hbm[11]
    evidence_ref, out_ref = refs[14:16]
    local = refs[16:27]
    (
        images_ref,
        defocus_ref,
        class_ref,
        rotation_ref,
        shift_ref,
        owner_ref,
        noise_ref,
        prior_ref,
        pair_ref,
        table_ref,
        spread_ref,
    ) = local
    (
        turn_ref,
        bend_ref,
        sides,
        held,
        joined,
        base,
        folded,
        shifted,
        picked_rows,
        rotated,
        rotated_low,
        cross_a,
        cross_b,
        unturned,
        stat_send,
        stats,
        part_send,
        parts,
        load_sem,
        ref_ssem,
        ref_rsem,
        stat_ssem,
        stat_rsem,
        part_ssem,
        part_rsem,
    ) = refs[27:]
    my_blk = lax.axis_index("blk")
    my_grp = lax.axis_index("grp")
    rows = images_ref.shape[0]
    own = refs_hbm.shape[0]
    classes = own * blk_size
    half_rows = classes * BEND

    loads = [
        pltpu.make_async_copy(source, place, load_sem.at[number])
        for number, (source, place) in enumerate(
            zip(hbm, local + (held.at[my_blk], turn_ref, bend_ref))
        )
    ]
    for load in loads:
        load.start()

    barrier = pltpu.get_barrier_semaphore()
    for d in range(1, blk_size):
        pl.semaphore_signal(
            barrier, inc=1, device_id={"blk": lax.rem(my_blk + d, blk_size)}, device_id_type=MESH
        )
    for d in range(1, grp_size):
        pl.semaphore_signal(
            barrier, inc=1, device_id={"grp": lax.rem(my_grp + d, grp_size)}, device_id_type=MESH
        )
    pl.semaphore_wait(barrier, blk_size + grp_size - 2)

    def ref_copy(d):
        return pltpu.make_async_remote_copy(
            src_ref=refs_hbm,
            dst_ref=held.at[my_blk],
            send_sem=ref_ssem.at[d],
            recv_sem=ref_rsem.at[d],
            device_id={"blk": lax.rem(my_blk + d, blk_size)},
            device_id_type=MESH,
        )

    for d in range(1, blk_size):
        ref_copy(d).start()

    for load in loads:
        load.wait()
    sides[...] = jnp.zeros(sides.shape, F32)
    sides[0:1, :CYCLES] = noise_ref[...]
    sides[8:9, :CYCLES] = prior_ref[...]
    sides[16:17, :classes] = owner_ref[...].astype(F32)

    rotation = rotation_ref[...]
    local_class = class_ref[...] - my_grp * classes
    member = (local_class >= 0) & (local_class < classes)
    target = jnp.where(member, rotation % BEND * classes + local_class, -1)
    side = jnp.where(rotation < BEND, 1.0, -1.0)
    wide_row = lax.broadcasted_iota(jnp.int32, (LANES, rows), 0)
    slot = jnp.dot(
        sides[16:24, :].astype(BF16),
        jnp.where(wide_row == local_class, 1.0, 0.0).astype(BF16),
        preferred_element_type=F32,
    )[0:1].astype(jnp.int32)
    slot = jnp.where(member, rotation % 8 * classes + slot, -1)

    cycle = lax.broadcasted_iota(jnp.int32, (32, rows), 0)
    frequency = (cycle.astype(F32) + 1.0) / CYCLES
    tall = jnp.where(
        cycle < CYCLES, -jnp.sin(defocus_ref[...] * (frequency * frequency) + 0.15), 0.0
    )
    empty = jnp.zeros((32, rows), F32)
    pieces = [piece.astype(F32) for piece in split3(tall)]
    packed = jnp.concatenate(pieces + [empty], axis=0).T.astype(BF16)
    contrast = jnp.concatenate([tall, empty, empty, empty], axis=0).T
    marks = jnp.where((wide_row % 16 == shift_ref[...]) & (wide_row < 48), 1.0, 0.0)
    marks = jnp.where((wide_row == 48) & (rotation >= 16), 1.0, marks)
    marks = jnp.where((wide_row == 49) & (rotation % 16 >= 8), 1.0, marks).T

    spread = spread_ref[...]
    wide = jnp.dot(packed, spread, preferred_element_type=F32)
    images = images_ref[...].astype(F32)
    base[:, :HALF] = images[:, :HALF] * wide
    base[:, HALF:] = images[:, HALF:] * wide

    lane = lax.broadcasted_iota(jnp.int32, (rows, LANES), 1)
    score_unit = math.log2(math.e) / math.sqrt(FEAT)
    noise_row = sides[0:8, :] * score_unit
    wide_noise = widen(sides[0:8, :], spread)[0:1]

    def weighted(column, part):
        at = column * LANES
        first = part * HALF + at
        scaled = base[:, first : first + LANES] * wide_noise[:, at : at + LANES]
        return scaled.astype(BF16).astype(F32)

    for j in range(FOLDS):
        for part in range(2):
            even, odd = fold_half(weighted(j, part), weighted(j + FOLDS, part), lane)
            place = part * FOLDED + j * LANES
            folded[:, place : place + LANES] = even
            folded[:, HALF + place : HALF + place + LANES] = odd

    def shift_rows(step, carry):
        start = pl.multiple_of(step * 16, 16)
        here = pl.ds(start, 16)
        for column in range(FOLDS):
            begin = column * LANES
            at = [slice(begin + n * FOLDED, begin + n * FOLDED + LANES) for n in range(4)]
            even_re, even_im, odd_re, odd_im = [folded[here, place] for place in at]
            for place, value in zip(at, (even_re, even_im, odd_re, odd_im)):
                shifted[SHIFTS // 2, here, place] = value.astype(BF16)
            for number, (first, second) in enumerate(PAIRS):
                cos_row = pair_ref[number : number + 1, at[0]]
                sin_row = pair_ref[4 + number : 5 + number, at[0]]
                for place, still, moved in (
                    (at[0], even_re, odd_im),
                    (at[1], even_im, -odd_re),
                    (at[2], odd_re, even_im),
                    (at[3], odd_im, -even_re),
                ):
                    left = cos_row * still
                    right = sin_row * moved
                    shifted[first, here, place] = (left + right).astype(BF16)
                    shifted[second, here, place] = (left - right).astype(BF16)
        return carry

    lax.fori_loop(0, rows // 16, shift_rows, 0)

    for d in range(1, blk_size):
        ref_copy(d).wait_recv()
    for b in range(blk_size):
        joined[b * own : (b + 1) * own, :] = held[b]
    whole_refs = joined[...]
    class_lane = lax.broadcasted_iota(jnp.int32, (classes, LANES), 1)
    evens, odds = [], []
    for part in range(2):
        scaled = whole_refs[:, part * HALF : (part + 1) * HALF] * (0.5 * score_unit)
        for j in range(FOLDS):
            even, odd = fold_half(
                scaled[:, j * LANES : (j + 1) * LANES],
                scaled[:, FOLDED + j * LANES : FOLDED + (j + 1) * LANES],
                class_lane,
            )
            evens.append(even)
            odds.append(odd)
    stacks = [jnp.concatenate(pieces, axis=0) for pieces in (evens, odds)]
    highs = [stack.astype(BF16) for stack in stacks]
    lows = [(stack - high.astype(F32)).astype(BF16) for stack, high in zip(stacks, highs)]

    def rotate(sources, place_ref):
        for r in range(0, BEND, 2):
            for part in range(2):
                begin = (part * BEND + r) * LANES
                spun = jnp.dot(
                    sources[part],
                    bend_ref[:, begin : begin + 2 * LANES],
                    preferred_element_type=F32,
                ).astype(BF16)
                for e in range(2):
                    for j in range(2 * FOLDS):
                        place = part * HALF + j * LANES
                        place_ref[
                            (r + e) * classes : (r + e + 1) * classes, place : place + LANES
                        ] = spun[j * classes : (j + 1) * classes, e * LANES : (e + 1) * LANES]

    rotate(highs, rotated)
    square = whole_refs[:, :HALF] * whole_refs[:, :HALF] + whole_refs[:, HALF:] * whole_refs[:, HALF:]
    power = sum(
        lax.dot_general(piece, spread, NT, preferred_element_type=F32) for piece in split3(square)
    )
    penalty = jnp.dot(
        power * (noise_row[0:1] * 0.5),
        jnp.concatenate([tall * tall, empty, empty, empty], axis=0),
        precision=lax.Precision.HIGHEST,
        preferred_element_type=F32,
    )

    def score(t, cross, turned_refs):
        for part in range(2):
            cross[part * half_rows : (part + 1) * half_rows, :] = lax.dot_general(
                turned_refs[:, part * HALF : (part + 1) * HALF],
                shifted[t, :, part * HALF : (part + 1) * HALF],
                NT,
                preferred_element_type=F32,
            )

    def both(cross, r):
        even = cross[r * classes : (r + 1) * classes, :]
        odd = cross[half_rows + r * classes : half_rows + (r + 1) * classes, :]
        return even, odd

    def fold(cross, running):
        peak, total = running
        even, odd = both(cross, 0)
        most = even + jnp.abs(odd)
        for r in range(1, BEND):
            even, odd = both(cross, r)
            most = jnp.maximum(most, even + jnp.abs(odd))
        new_peak = jnp.maximum(peak, jnp.max(most - penalty, axis=0, keepdims=True))
        lowered = penalty + new_peak
        added = jnp.zeros((classes, rows), F32)
        for r in range(BEND):
            even, odd = both(cross, r)
            even = even - lowered
            added = added + (jnp.exp2(even + odd) + jnp.exp2(even - odd))
        total = total * jnp.exp2(peak - new_peak) + jnp.sum(added, axis=0, keepdims=True)
        return new_peak, total

    def visit(step, running):
        score(2 * step + 1, cross_b, rotated)
        running = fold(cross_a, running)
        score(2 * step + 2, cross_a, rotated)
        return fold(cross_b, running)

    score(0, cross_a, rotated)
    running = lax.fori_loop(
        0,
        SHIFTS // 2,
        visit,
        (jnp.full((1, rows), -1e30, F32), jnp.zeros((1, rows), F32)),
    )
    peak, total = fold(cross_a, running)

    stat_send[...] = jnp.concatenate([peak, total, jnp.zeros((6, rows), F32)], axis=0)

    def stat_copy(d):
        return pltpu.make_async_remote_copy(
            src_ref=stat_send,
            dst_ref=stats.at[my_grp],
            send_sem=stat_ssem.at[d],
            recv_sem=stat_rsem.at[d],
            device_id={"grp": lax.rem(my_grp + d, grp_size)},
            device_id_type=MESH,
        )

    for d in range(1, grp_size):
        stat_copy(d).start()
    stats[my_grp] = stat_send[...]

    turns = jnp.dot(marks.astype(BF16), table_ref[...], preferred_element_type=F32)
    far_turn = jnp.broadcast_to(marks[:, 48:49], (rows, LANES)) > 0.5
    near_turn = jnp.broadcast_to(marks[:, 49:50], (rows, LANES)) > 0.5

    def keep(part, first):
        high = part.astype(BF16)
        low = (part - high.astype(F32)).astype(BF16)
        picked_rows[:rows, first : first + LANES] = high
        picked_rows[rows : 2 * rows, first : first + LANES] = low
        picked_rows[2 * rows :, first : first + LANES] = high

    keep(contrast * contrast, FEAT)
    for j in range(FOLDS):
        moved = []
        for column in (j, j + FOLDS):
            at_re = slice(column * LANES, (column + 1) * LANES)
            at_im = slice(HALF + column * LANES, HALF + (column + 1) * LANES)
            real = base[:, at_re]
            imag = base[:, at_im]
            for part, at in (
                (turns[:, at_re] * real + turns[:, at_im] * imag, at_re),
                (turns[:, at_re] * imag - turns[:, at_im] * real, at_im),
            ):
                part = jnp.where(far_turn, turn_left(part, 16, lane), part)
                part = jnp.where(near_turn, turn_left(part, 8, lane), part)
                keep(part, at.start)
            real = weighted(column, 0)
            imag = weighted(column, 1)
            moved.append(turns[:, at_re] * real + turns[:, at_im] * imag)
            moved.append(turns[:, at_re] * imag - turns[:, at_im] * real)
        for part in range(2):
            place = part * FOLDED + j * LANES
            for number, value in enumerate(fold_half(moved[part], moved[part + 2], lane)):
                first = number * HALF + place
                high = value.astype(BF16)
                shifted[SHIFTS, :, first : first + LANES] = high
                shifted[SHIFTS + 1, :, first : first + LANES] = (
                    value - high.astype(F32)
                ).astype(BF16)
    rotate(lows, rotated_low)
    score(SHIFTS, cross_b, rotated)
    score(SHIFTS, cross_a, rotated_low)
    class_row = lax.broadcasted_iota(jnp.int32, (classes, rows), 0)

    def pick(cross, chosen_sum, offset):
        for r in range(BEND):
            even, odd = both(cross, r)
            chosen_sum = chosen_sum + jnp.where(
                class_row + r * classes == target, even + side * odd - offset, 0.0
            )
        return chosen_sum

    chosen_sum = pick(cross_b, jnp.zeros((classes, rows), F32), penalty)
    score(SHIFTS + 1, cross_b, rotated)
    chosen_sum = pick(cross_a, chosen_sum, 0.0)
    chosen_sum = pick(cross_b, chosen_sum, 0.0)
    picked = jnp.sum(chosen_sum, axis=0, keepdims=True)

    for d in range(1, grp_size):
        stat_copy(d).wait_recv()
    peaks = [stats[g][0:1] for g in range(grp_size)]
    totals = [stats[g][1:2] for g in range(grp_size)]
    top = functools.reduce(jnp.maximum, peaks)
    whole = sum(t * jnp.exp2(p - top) for p, t in zip(peaks, totals))
    log_sum = top + jnp.log2(whole)
    orients = classes * grp_size * ANGLES * SHIFTS
    evidence_ref[...] = log_sum * math.log(2.0) - math.log(orients)
    weight = jnp.where(target >= 0, jnp.exp2(jnp.minimum(picked - log_sum, 16.0)) * orients, 0.0)

    turned_row = lax.broadcasted_iota(jnp.int32, (8 * classes, rows), 0)
    placed = jnp.where(turned_row == slot, weight, 0.0)
    placed_high = placed.astype(BF16)
    placed_low = (placed - placed_high.astype(F32)).astype(BF16)
    left = jnp.concatenate([placed_high, placed_high, placed_low], axis=1)
    count = CHUNKS * classes
    for j in range(0, CHUNKS, 2):
        block = jnp.dot(
            left, picked_rows[:, j * LANES : (j + 2) * LANES], preferred_element_type=F32
        )
        high = block.astype(BF16)
        low = (block - high.astype(F32)).astype(BF16)
        for e in range(2):
            first = (j + e) * classes
            for r in range(8):
                at = (slice(r * classes, (r + 1) * classes), slice(e * LANES, (e + 1) * LANES))
                unturned[first : first + classes, r * LANES : (r + 1) * LANES] = high[at]
                unturned[count + first : count + first + classes, r * LANES : (r + 1) * LANES] = (
                    low[at]
                )
    block = jnp.dot(left, picked_rows[:, FEAT:], preferred_element_type=F32)
    denominator = block[0:classes]
    for r in range(1, 8):
        denominator = denominator + block[r * classes : (r + 1) * classes]
    sums = lax.dot_general(unturned[...], turn_ref[...], NT, preferred_element_type=F32)
    sums = sums[:count] + sums[count:]
    for b in range(blk_size):
        for j in range(CHUNKS):
            part_send[b, :, j * LANES : (j + 1) * LANES] = sums[
                j * classes + b * own : j * classes + (b + 1) * own
            ]
        part_send[b, :, FEAT:] = denominator[b * own : (b + 1) * own]

    def part_copy(d):
        peer = lax.rem(my_blk + d, blk_size)
        return pltpu.make_async_remote_copy(
            src_ref=part_send.at[peer],
            dst_ref=parts.at[d],
            send_sem=part_ssem.at[d],
            recv_sem=part_rsem.at[d],
            device_id={"blk": peer},
            device_id_type=MESH,
        )

    for d in range(1, blk_size):
        part_copy(d).start()
    gathered = part_send[my_blk]
    for d in range(1, blk_size):
        part_copy(d).wait_recv()
        gathered = gathered + parts[d]
    lower = gathered[:, FEAT:] + sides[8:9, :]
    lower = jnp.concatenate([lower, jnp.ones((8 - own, LANES), F32)], axis=0)
    lane8 = lax.broadcasted_iota(jnp.int32, (8, LANES), 1)
    lower = widen(jnp.where(lane8 < CYCLES, lower, 0.0), spread)[:own]
    out_ref[:, :HALF] = gathered[:, :HALF] / lower
    out_ref[:, HALF:] = gathered[:, HALF:FEAT] / lower
    for d in range(1, blk_size):
        ref_copy(d).wait_send()
        part_copy(d).wait_send()
    for d in range(1, grp_size):
        stat_copy(d).wait_send()


def pass_on(first_in, second_in, first_out, second_out, sem):
    copies = [
        pltpu.make_async_copy(first_in, first_out, sem.at[0]),
        pltpu.make_async_copy(second_in, second_out, sem.at[1]),
    ]
    for copy in copies:
        copy.start()
    for copy in copies:
        copy.wait()


def shards(images, defocus, class_id, rotation_id, shift_id, references, owner, inv_noise, prior):
    rows = images.shape[0]
    own = references.shape[1]
    blk_size = lax.axis_size("blk")
    grp_size = lax.axis_size("grp")
    classes = owner.shape[1]
    turned = classes * ANGLES
    operands = [
        images,
        defocus.reshape(1, rows),
        class_id.reshape(1, rows),
        rotation_id.reshape(1, rows),
        shift_id.reshape(1, rows),
        owner,
        inv_noise.reshape(1, CYCLES),
        prior.reshape(1, CYCLES),
        *[jnp.asarray(table) for table in constant_tables()[:3]],
        references[0],
        *[jnp.asarray(table) for table in constant_tables()[3:]],
    ]
    vmem = pl.BlockSpec(memory_space=pltpu.VMEM)
    whole = pl.BlockSpec(memory_space=pl.ANY)
    outs = (
        jax.ShapeDtypeStruct((1, rows), F32),
        jax.ShapeDtypeStruct((own, FEAT), F32),
    )
    evidence, new_refs = pl.pallas_call(
        functools.partial(kernel, blk_size, grp_size),
        out_shape=outs,
        in_specs=[whole] * 14,
        out_specs=(vmem, vmem),
        scratch_shapes=[
            *[pltpu.VMEM(operand.shape, operand.dtype) for operand in operands[:11]],
            pltpu.VMEM(operands[12].shape, BF16),
            pltpu.VMEM(operands[13].shape, BF16),
            pltpu.VMEM((24, LANES), F32),
            pltpu.VMEM((blk_size, own, FEAT), F32),
            pltpu.VMEM((classes, FEAT), F32),
            pltpu.VMEM((rows, FEAT), F32),
            pltpu.VMEM((rows, FEAT), F32),
            pltpu.VMEM((SHIFTS + 2, rows, FEAT), BF16),
            pltpu.VMEM((3 * rows, FEAT + LANES), BF16),
            pltpu.VMEM((turned // 2, FEAT), BF16),
            pltpu.VMEM((turned // 2, FEAT), BF16),
            pltpu.VMEM((turned, rows), F32),
            pltpu.VMEM((turned, rows), F32),
            pltpu.VMEM((2 * CHUNKS * classes, 8 * LANES), BF16),
            pltpu.VMEM((8, rows), F32),
            pltpu.VMEM((grp_size, 8, rows), F32),
            pltpu.VMEM((blk_size, own, FEAT + LANES), F32),
            pltpu.VMEM((blk_size, own, FEAT + LANES), F32),
            pltpu.SemaphoreType.DMA((14,)),
            pltpu.SemaphoreType.DMA((blk_size,)),
            pltpu.SemaphoreType.DMA((blk_size,)),
            pltpu.SemaphoreType.DMA((grp_size,)),
            pltpu.SemaphoreType.DMA((grp_size,)),
            pltpu.SemaphoreType.DMA((blk_size,)),
            pltpu.SemaphoreType.DMA((blk_size,)),
        ],
        compiler_params=pltpu.CompilerParams(
            collective_id=0, has_side_effects=True, vmem_limit_bytes=60 * 1024 * 1024
        ),
    )(*operands)
    evidence, new_refs = pl.pallas_call(
        pass_on,
        out_shape=outs,
        in_specs=[whole] * 2,
        out_specs=(whole, whole),
        scratch_shapes=[pltpu.SemaphoreType.DMA((2,))],
    )(evidence, new_refs)
    return (evidence[0], new_refs[None])


def solution(mesh):
    in_specs = (
        P("blk", None),
        P("blk"),
        P("blk", None),
        P("blk"),
        P("blk"),
        P("grp", "blk", None),
        P("grp", None),
        P(),
        P(),
    )
    out_specs = (P("blk"), P("grp", "blk", None))
    return jax.shard_map(shards, mesh=mesh, in_specs=in_specs, out_specs=out_specs, check_vma=False)
```
